256 devices in a mesh: slab: 16 (over z_hi, y), tp: 4 (over x), band: 4 (over z_lo, core).
Axes of the slice: x: 4, y: 4, z: 8 (z_hi: 4, z_lo: 2; z = z_hi * 2 + z_lo), core: 2. Of those that a mesh axis runs over, the one named last changes fastest.
Arguments:
- tokens: bfloat16 [24576, 3072], P(('slab', 'band'), 'tp'), may hold values from -6 to 6
- w_qkv: bfloat16 [3072, 3, 3072], P('band', None, 'tp'), may hold values from -0.109375 to 0.109375
- w_out: bfloat16 [3072, 3072], P('tp'), may hold values from -0.109375 to 0.109375
- shift: float32 [3072], replicated, may hold values from -3 to 3
- scale: float32 [3072], replicated, may hold values from -0.9 to 0.9
- gate: float32 [3072], P('tp'), may hold values from 0.5 to 2
- q_gain: float32 [128], replicated, may hold values from 0.5 to 5.5
- k_gain: float32 [128], replicated, may hold values from 0.5 to 5.5
- tile_ids: int32 [192, 14], P(('slab', 'band')), may hold values from 0 to 191, as said below
- key_counts: int32 [192], P(('slab', 'band')), may hold values from 1 to 14, as said below
Outputs:
- update: bfloat16 [24576, 3072], P(('slab', 'band'), 'tp')
The draws below stay inside these ranges and needn't reach their ends.
Inputs may be any that keep to these rules, and one draw needn't show every extreme that they name: `tile_ids`: row q's first key_counts[q] entries are distinct tiles, the first being q itself, whose time index (tile // 12), row index ((tile // 3) % 4) and column index (tile % 3) each differ from q's by at most one; the remaining entries equal q. `key_counts`: 14 is reached in every draw.
All inputs are finite; a program needn't handle non-finite values.
Results may differ from the reference program's by a relative error of at most 0.014.
The reference program's roundings to bfloat16 on the way (of `normed`, `queries`, `keys`, `values`, `probs` and `attended`) count: a program that leaves them out, or rounds other values in their place, can miss the bound.
Values may be sent and summed in bfloat16 or wider, within the bound.
No kernel may reach another device: no remote copies, remote signals or barrier semaphores. Data moves between devices by JAX's collectives and lax.ppermute only.
A program may use at most 128 MiB of HBM per device.

```python
import jax
import jax.numpy as jnp
from jax import lax

D = 3072
HD = 128
HEADS = 24
TC = 3
TILE = 128
WIN = 14
TT = 16
TR = 4
NTILES = 192
TOKENS = 24576


def pattern_tables(key):
    local_key = jax.random.fold_in(key, 71)
    first_key, second_key = jax.random.split(local_key)
    tile = jnp.arange(NTILES, dtype=jnp.int32)
    time_pos = tile // (TR * TC)
    row_pos = tile // TC % TR
    column_pos = tile % TC
    offset = jnp.arange(27, dtype=jnp.int32)
    time_near = time_pos[:, None] + offset[None, :] // 9 - 1
    row_near = row_pos[:, None] + offset[None, :] // 3 % 3 - 1
    column_near = column_pos[:, None] + offset[None, :] % 3 - 1
    inside = (time_near >= 0) & (time_near < TT) & (row_near >= 0) & (row_near < TR)
    inside = inside & (column_near >= 0) & (column_near < TC)
    near_id = (time_near * TR + row_near) * TC + column_near
    noise = jax.random.randint(first_key, (NTILES, 27), 0, 2 ** 20)
    priority = jnp.where(offset[None, :] == 13, 2 ** 30, 0) + inside.astype(jnp.int32) * 2 ** 26 + noise * 32 + offset[None, :]
    unused, order = lax.top_k(priority, WIN)
    chosen = jnp.take_along_axis(near_id, order, axis=1)
    upper = jnp.minimum(jnp.sum(inside.astype(jnp.int32), axis=1), WIN)
    number = jax.random.randint(second_key, (NTILES,), 1, upper + 1)
    number = jnp.where(tile == TC + 1, WIN, number).astype(jnp.int32)
    slot_ids = jnp.arange(WIN, dtype=jnp.int32)
    listed = jnp.where(slot_ids[None, :] < number[:, None], chosen, tile[:, None])
    return (listed.astype(jnp.int32), number)


def draw_tile_ids(key, part):
    return pattern_tables(key)[0]


def draw_key_counts(key, part):
    return pattern_tables(key)[1]


def gain_draw(key):
    return jax.random.uniform(key, (HD,), jnp.float32, 0.6, 1.6)


def draw_q_gain(key, part):
    return gain_draw(jax.random.fold_in(key, 11))


def draw_k_gain(key, part):
    return gain_draw(jax.random.fold_in(key, 13))


def block_scale(rng, dims, cuts, least, high):
    loudness = 1.0
    for axis_at, blocks in cuts:
        draws = jax.random.uniform(jax.random.fold_in(jax.random.fold_in(rng, 6), axis_at), (blocks,), jnp.float32, least / len(cuts), high / len(cuts))
        loudness = loudness * jnp.repeat(jnp.exp(draws), dims[axis_at] // blocks).reshape((-1,) + (1,) * (len(dims) - 1 - axis_at))
    return loudness


def normal_values(key, shape, scale, most, pieces=(), kind=jnp.bfloat16):
    entries = scale * jax.random.normal(key, shape, jnp.float32)
    if pieces:
        entries = entries * block_scale(key, shape, pieces, -0.22, 0.18)
    return jnp.clip(entries, -most, most).astype(kind)


def setup_inputs(seed: int = 0) -> dict:
    key_list = jax.random.split(jax.random.key(seed), 11)
    return {
        "tokens": normal_values(key_list[0], (TOKENS, D), 1.0, 6.0, ((0, 64), (1, 4))),
        "w_qkv": normal_values(key_list[1], (D, 3, D), D ** -0.5, 0.109375, ((0, 4), (2, 4))),
        "w_out": normal_values(key_list[2], (D, D), D ** -0.5, 0.109375, ((0, 4),)),
        "shift": normal_values(key_list[3], (D,), 0.5, 3.0, (), jnp.float32),
        "scale": normal_values(key_list[4], (D,), 0.3, 0.9, (), jnp.float32),
        "gate": jnp.clip(0.5 + 1.5 * jax.random.uniform(key_list[5], (D,), jnp.float32) ** block_scale(key_list[5], (D,), ((0, 4),), -0.2, 0.2), 0.5, 2.0),
        "q_gain": draw_q_gain(jax.random.fold_in(key_list[10], 71), 0),
        "k_gain": draw_k_gain(jax.random.fold_in(key_list[10], 71), 0),
        "tile_ids": draw_tile_ids(jax.random.fold_in(key_list[10], 71), 0),
        "key_counts": draw_key_counts(jax.random.fold_in(key_list[10], 71), 0),
    }


def head_norm(part, gain):
    squares = lax.optimization_barrier(jnp.mean(part * part, axis=-1, keepdims=True))
    return (part * lax.rsqrt(squares + 1e-06) * gain).astype(jnp.bfloat16)

def reference(tokens, w_qkv, w_out, shift, scale, gate, q_gain, k_gain, tile_ids, key_counts):
    floats = tokens.astype(jnp.float32)
    center = lax.optimization_barrier(jnp.mean(floats, axis=-1, keepdims=True))
    spread = lax.optimization_barrier(jnp.mean((floats - center) ** 2, axis=-1, keepdims=True))
    normed = ((floats - center) * lax.rsqrt(spread + 1e-06) * (1.0 + scale) + shift).astype(jnp.bfloat16)
    projected = jnp.dot(normed, w_qkv.reshape(D, 3 * D), preferred_element_type=jnp.float32)
    projected = projected.reshape(TOKENS, 3, HEADS, HD)
    queries = head_norm(projected[:, 0], q_gain)
    keys = head_norm(projected[:, 1], k_gain)
    values = projected[:, 2].astype(jnp.bfloat16)
    query_tiles = queries.reshape(NTILES, TILE, HEADS, HD)
    key_tiles = keys.reshape(NTILES, TILE, HEADS, HD)
    value_tiles = values.reshape(NTILES, TILE, HEADS, HD)
    inverse = 1.0 / HD ** 0.5

    def one_tile(items):
        listed, number, query = items
        near_keys = jnp.take(key_tiles, listed, axis=0).astype(jnp.float32)
        near_values = jnp.take(value_tiles, listed, axis=0).astype(jnp.float32)
        scores = jnp.einsum('qhd,wkhd->hqwk', query.astype(jnp.float32), near_keys) * inverse
        allowed = (jnp.arange(WIN) < number)[None, None, :, None]
        scores = jnp.where(allowed, scores, -1e+30)
        top = lax.optimization_barrier(jnp.max(scores, axis=(2, 3), keepdims=True))
        weights = jnp.exp(scores - top)
        probs = (weights / lax.optimization_barrier(jnp.sum(weights, axis=(2, 3), keepdims=True))).astype(jnp.bfloat16)
        result = jnp.einsum('hqwk,wkhd->qhd', probs.astype(jnp.float32), near_values)
        return result.astype(jnp.bfloat16)
    attended = lax.map(one_tile, (tile_ids, key_counts, query_tiles)).reshape(TOKENS, D)
    product = jnp.dot(attended, w_out, preferred_element_type=jnp.float32)
    return (gate * product).astype(jnp.bfloat16)
```

```python
import functools

import jax
import jax.numpy as jnp
from jax import lax
from jax.experimental import pallas as pl
from jax.experimental.pallas import tpu as pltpu
from jax.sharding import PartitionSpec as P

HD = 128
HH = 3
HF = HH * HD
TILE = 128
WIN = 14
ROWS = 384
FS = 768
D = 3072
F32 = jnp.float32
BF16 = jnp.bfloat16
ANY = pl.BlockSpec(memory_space=pl.ANY)
VM = pl.BlockSpec(memory_space=pltpu.VMEM)
SM = pl.BlockSpec(memory_space=pltpu.SMEM)
VMEM_LIMIT = 56 * 1024 * 1024

RIGHT = [(i, (i + 1) % 4) for i in range(4)]
LEFT = [(i, (i + 3) % 4) for i in range(4)]
ACROSS = [(i, (i + 2) % 4) for i in range(4)]
CORE = [(b, b ^ 1) for b in range(4)]
PAIR = [(b, b ^ 2) for b in range(4)]
LATER = [(i, i + 1) for i in range(15)]
EARLIER = [(i + 1, i) for i in range(15)]


def other_side():
    pairs = []
    for slab in range(16):
        for band in range(4):
            z = (slab // 4) * 2 + band // 2
            z = (z - 1) % 8 if z % 2 == 0 else (z + 1) % 8
            pairs.append((slab * 4 + band, (z // 2 * 4 + slab % 4) * 4 + z % 2 * 2 + band % 2))
    return pairs


OUTER = other_side()


def qkv_kernel(meta, x0, xl, xr, xt, xb, wo, wc, wza, wzb, wca, wcb, scale, shift, qg, kg,
               q_ref, kv_ref, wbuf, nbuf, sems):
    copies = []

    def put(src, dst, n):
        cp = pltpu.make_async_copy(src, dst, sems.at[n])
        cp.start()
        copies.append(cp)

    def krows(k):
        return pl.ds(pl.multiple_of(meta[4 + k] * FS, FS), FS)

    put(wo, wbuf.at[:, krows(0)], 0)
    put(wc, wbuf.at[:, krows(1)], 1)
    put(wza, wbuf.at[0:1, krows(2)], 2)
    put(wzb, wbuf.at[1:3, krows(2)], 3)
    put(wca, wbuf.at[0:1, krows(3)], 4)
    put(wcb, wbuf.at[1:3, krows(3)], 5)

    step = 16

    def rows_of(far, base):
        def body(i, carry):
            r = pl.multiple_of(base + i * step, step)
            f = pl.multiple_of(i * step, step)
            parts = [ref[pl.ds(r, step), :].astype(F32) for ref in (x0, xl, xr)]
            parts.append(far[pl.ds(f, step), :].astype(F32))
            total = sum(jnp.sum(p, axis=-1, keepdims=True) for p in parts)
            center = total * (1.0 / D)
            parts = [p - center for p in parts]
            spread = sum(jnp.sum(p * p, axis=-1, keepdims=True) for p in parts) * (1.0 / D)
            inv = lax.rsqrt(spread + 1e-06)
            for k, p in enumerate(parts):
                at = meta[k]
                y = p * inv * (1.0 + scale[at]) + shift[at]
                nbuf[pl.ds(r, step), pl.ds(pl.multiple_of(at * FS, FS), FS)] = y.astype(BF16)
            return carry

        lax.fori_loop(0, ROWS // 2 // step, body, 0)

    rows_of(xt, 0)
    rows_of(xb, ROWS // 2)
    for cp in copies:
        cp.wait()
    for p in (1, 2, 0):
        acc = jnp.dot(nbuf[...], wbuf[p], preferred_element_type=F32)
        if p == 2:
            kv_ref[:, HF:] = acc.astype(BF16)
            continue
        gain = kg if p else qg
        for h in range(HH):
            part = acc[:, h * HD:(h + 1) * HD]
            squares = jnp.mean(part * part, axis=-1, keepdims=True)
            out = (part * lax.rsqrt(squares + 1e-06) * gain[...]).astype(BF16)
            if p:
                kv_ref[:, h * HD:(h + 1) * HD] = out
            else:
                q_ref[:, h * HD:(h + 1) * HD] = out


def qkv(meta, xs, ws, scale, shift, qg, kg):
    return pl.pallas_call(
        qkv_kernel,
        out_shape=(jax.ShapeDtypeStruct((ROWS, HF), BF16), jax.ShapeDtypeStruct((ROWS, 2 * HF), BF16)),
        in_specs=[SM] + [VM] * 5 + [ANY] * 6 + [VM] * 4,
        out_specs=(VM, VM),
        scratch_shapes=[
            pltpu.VMEM((3, D, HF), BF16),
            pltpu.VMEM((ROWS, D), BF16),
            pltpu.SemaphoreType.DMA((6,)),
        ],
        compiler_params=pltpu.CompilerParams(vmem_limit_bytes=VMEM_LIMIT),
        cost_estimate=pl.CostEstimate(flops=2 * ROWS * D * 3 * HF, bytes_accessed=10 * 2**20, transcendentals=0),
        name="qkv",
    )(meta, *xs, *ws, scale, shift, qg, kg)


def attend_kernel(meta, ids, q_ref, *rest):
    pieces = rest[:12]
    o_ref, kv, sems = rest[12:]
    copies = []
    for n, piece in enumerate(pieces):
        cp = pltpu.make_async_copy(piece, kv.at[pl.ds(n * ROWS, ROWS)], sems.at[n])
        cp.start()
        copies.append(cp)
    for cp in copies:
        cp.wait()
    slab, side, core = meta[8], meta[9], meta[10]

    def place(tile):
        dt = jnp.clip(tile // 12 - slab + 1, 0, 2)
        row = (tile // 3) % 4
        r = jnp.abs(row // 2 - side)
        cr = jnp.abs(row % 2 - core)
        return (((dt * 2 + r) * 2 + cr) * 3 + tile % 3) * TILE

    factor = 1.0 / HD**0.5

    def run(qt, count, slots):
        spots = [pl.multiple_of(place(ids[qt, j]), TILE) for j in range(slots)]
        rows = pl.ds(pl.multiple_of(qt * TILE, TILE), TILE)
        for h in range(HH):
            cols = slice(h * HD, (h + 1) * HD)
            vcols = slice(HF + h * HD, HF + (h + 1) * HD)
            q = q_ref[rows, cols]
            scores = []
            for j in range(0, slots, 2):
                k = jnp.concatenate([kv[pl.ds(spots[j], TILE), cols], kv[pl.ds(spots[j + 1], TILE), cols]], axis=0)
                s = lax.dot_general(q, k, (((1,), (1,)), ((), ())), preferred_element_type=F32)
                for i in range(2):
                    live = jnp.where(j + i < count, 0.0, -1e30)
                    scores.append(s[:, i * TILE:(i + 1) * TILE] * factor + live)
            top = functools.reduce(jnp.maximum, scores)
            top = jnp.max(top, axis=-1, keepdims=True)
            weights = [jnp.exp(s - top) for s in scores]
            total = functools.reduce(jnp.add, weights)
            inv = 1.0 / jnp.sum(total, axis=-1, keepdims=True)
            acc = None
            for j in range(0, slots, 2):
                p = jnp.concatenate([(weights[j] * inv).astype(BF16), (weights[j + 1] * inv).astype(BF16)], axis=1)
                v = jnp.concatenate([kv[pl.ds(spots[j], TILE), vcols], kv[pl.ds(spots[j + 1], TILE), vcols]], axis=0)
                o = jnp.dot(p, v, preferred_element_type=F32)
                acc = o if acc is None else acc + o
            o_ref[rows, cols] = acc.astype(BF16)

    def tile_loop(qt, carry):
        count = ids[qt, WIN]
        lo = 0
        for slots in (4, 8, WIN):
            @pl.when((count > lo) & (count <= slots))
            def _(slots=slots):
                run(qt, count, slots)
            lo = slots
        return carry

    lax.fori_loop(0, ROWS // TILE, tile_loop, 0)


def attend(meta, ids, q, pieces):
    return pl.pallas_call(
        attend_kernel,
        out_shape=jax.ShapeDtypeStruct((ROWS, HF), BF16),
        in_specs=[SM, SM, VM] + [ANY] * 12,
        out_specs=VM,
        scratch_shapes=[
            pltpu.VMEM((12 * ROWS, 2 * HF), BF16),
            pltpu.SemaphoreType.DMA((12,)),
        ],
        compiler_params=pltpu.CompilerParams(vmem_limit_bytes=VMEM_LIMIT),
        cost_estimate=pl.CostEstimate(flops=4 * ROWS * WIN * TILE * HF, bytes_accessed=8 * 2**20,
                                      transcendentals=ROWS * WIN * TILE * HH),
        name="attend",
    )(meta, ids, q, *pieces)


def out_kernel(meta, *rest):
    att, wts, gate = rest[:10], rest[10:18], rest[18]
    o_ref, abuf, wbuf, sems = rest[19:]
    side, core = meta[9], meta[10]
    copies = []

    def put(src, dst):
        cp = pltpu.make_async_copy(src, dst, sems.at[len(copies)])
        cp.start()
        copies.append(cp)

    half = ROWS // 2
    for which in range(2):
        at = side if which == 0 else 1 - side
        a0, al, ar, top, bottom = att[which * 5:which * 5 + 5]
        put(a0, abuf.at[0, at])
        put(al, abuf.at[1, at])
        put(ar, abuf.at[2, at])
        put(top, abuf.at[3, at, pl.ds(0, half)])
        put(bottom, abuf.at[3, at, pl.ds(half, half)])
    for k in range(4):
        put(wts[2 * k], wbuf.at[k, core])
        put(wts[2 * k + 1], wbuf.at[k, 1 - core])
    for cp in copies:
        cp.wait()
    for r in range(0, ROWS, ROWS):
        acc = None
        for k in range(4):
            for h in range(2):
                o = jnp.dot(abuf[k, h, r:r + ROWS], wbuf[k, h], preferred_element_type=F32)
                acc = o if acc is None else acc + o
        o_ref[r:r + ROWS, :] = (acc * gate[...]).astype(BF16)


def out_proj(meta, att, wts, gate):
    return pl.pallas_call(
        out_kernel,
        out_shape=jax.ShapeDtypeStruct((ROWS, FS), BF16),
        in_specs=[SM] + [ANY] * 18 + [VM],
        out_specs=VM,
        scratch_shapes=[
            pltpu.VMEM((4, 2, ROWS, HF), BF16),
            pltpu.VMEM((4, 2, HF, FS), BF16),
            pltpu.SemaphoreType.DMA((18,)),
        ],
        compiler_params=pltpu.CompilerParams(vmem_limit_bytes=VMEM_LIMIT),
        cost_estimate=pl.CostEstimate(flops=2 * ROWS * D * FS, bytes_accessed=8 * 2**20, transcendentals=0),
        name="out_proj",
    )(meta, *att, *wts, gate)


def ring_gather(x):
    half = x.shape[0] // 2
    left = lax.ppermute(x, "tp", RIGHT)
    right = lax.ppermute(x, "tp", LEFT)
    top = lax.ppermute(left[:half], "tp", RIGHT)
    bottom = lax.ppermute(right[half:], "tp", LEFT)
    return x, left, right, top, bottom


def shards(tokens, w_qkv, w_out, shift, scale, gate, q_gain, k_gain, tile_ids, key_counts):
    tp = lax.axis_index("tp")
    slab = lax.axis_index("slab")
    band = lax.axis_index("band")
    side, core = band // 2, band % 2
    meta = jnp.stack([
        tp, (tp + 3) % 4, (tp + 1) % 4, (tp + 2) % 4,
        band, band ^ 1, band ^ 2, band ^ 3,
        slab, side, core, core,
    ]).astype(jnp.int32)

    swap = functools.partial(lax.ppermute, axis_name="band", perm=CORE)
    pair = functools.partial(lax.ppermute, axis_name="band", perm=PAIR)

    listed = jnp.concatenate([tile_ids, key_counts[:, None], key_counts[:, None]], axis=1)
    partner_listed = pair(listed)
    partner_tokens = pair(tokens)
    own_x = ring_gather(tokens)
    partner_x = ring_gather(partner_tokens)

    w = w_qkv.transpose(1, 0, 2)
    w_own = lax.dynamic_slice_in_dim(w, side * HF, HF, 2)
    w_away = lax.dynamic_slice_in_dim(w, (1 - side) * HF, HF, 2)
    w_za = pair(w_away[:1])
    w_zb = lax.ppermute(w_away[1:], ("slab", "band"), OUTER)
    w_core = swap(w_own)
    ws = (w_own, w_core, w_za, w_zb, swap(w_za), swap(w_zb))

    scale4, shift4 = scale.reshape(4, 1, FS), shift.reshape(4, 1, FS)
    qg, kg = q_gain.reshape(1, HD), k_gain.reshape(1, HD)

    def spread(kv):
        before = lax.ppermute(kv, "slab", LATER)
        after = lax.ppermute(kv, "slab", EARLIER)
        return [(x, swap(x)) for x in (before, kv, after)]

    own_q, own_kv = qkv(meta, own_x, ws, scale4, shift4, qg, kg)
    own_near = spread(own_kv)
    partner_q, partner_kv = qkv(meta, partner_x, ws, scale4, shift4, qg, kg)
    partner_near = spread(partner_kv)

    rows = lax.dynamic_slice_in_dim(w_out, core * HF, HF, 0)

    def cols(k):
        return lax.dynamic_slice_in_dim(rows, (tp + k) % 4 * FS, FS, 1)

    mine = lax.dynamic_slice_in_dim(w_out, tp * FS, FS, 1)
    w_mine = lax.dynamic_slice_in_dim(mine, core * HF, HF, 0)
    w_other = lax.dynamic_slice_in_dim(mine, (1 - core) * HF, HF, 0)
    w_left = lax.ppermute(cols(1), "tp", RIGHT)
    w_right = lax.ppermute(cols(3), "tp", LEFT)
    w_far = lax.ppermute(cols(2), "tp", ACROSS)
    wts = (w_mine, w_other, w_left, swap(w_left), w_right, swap(w_right), w_far, swap(w_far))

    pieces = []
    for t in range(3):
        for near in (own_near, partner_near):
            pieces.extend(near[t])
    away = attend(meta, partner_listed, partner_q, pieces)
    home = attend(meta, listed, own_q, pieces)
    back = pair(away)
    att = ring_gather(home) + ring_gather(back)
    return out_proj(meta, att, wts, gate.reshape(1, FS))


def solution(mesh):
    in_specs = (
        P(("slab", "band"), "tp"),
        P("band", None, "tp"),
        P("tp", None),
        P(),
        P(),
        P("tp"),
        P(),
        P(),
        P(("slab", "band"), None),
        P(("slab", "band")),
    )
    out_specs = P(("slab", "band"), "tp")
    return jax.shard_map(shards, mesh=mesh, in_specs=in_specs, out_specs=out_specs, check_vma=False)
```

```python
import functools

import jax
import jax.numpy as jnp
from jax import lax
from jax.experimental import pallas as pl
from jax.experimental.pallas import tpu as pltpu
from jax.sharding import PartitionSpec as P

HD = 128
HH = 3
HF = HH * HD
TILE = 128
WIN = 14
ROWS = 384
HALF = ROWS // 2
FS = 768
D = 3072
F32 = jnp.float32
BF16 = jnp.bfloat16
HBM = pl.BlockSpec(memory_space=pltpu.HBM)
ANY = pl.BlockSpec(memory_space=pl.ANY)
VM = pl.BlockSpec(memory_space=pltpu.VMEM)
SM = pl.BlockSpec(memory_space=pltpu.SMEM)

RIGHT = [(i, (i + 1) % 4) for i in range(4)]
LEFT = [(i, (i + 3) % 4) for i in range(4)]
ACROSS = [(i, (i + 2) % 4) for i in range(4)]
CORE = [(b, b ^ 1) for b in range(4)]
PAIR = [(b, b ^ 2) for b in range(4)]
LATER = [(i, i + 1) for i in range(15)]
EARLIER = [(i + 1, i) for i in range(15)]


def other_side():
    pairs = []
    for slab in range(16):
        for band in range(4):
            z = (slab // 4) * 2 + band // 2
            z = (z - 1) % 8 if z % 2 == 0 else (z + 1) % 8
            pairs.append((slab * 4 + band, (z // 2 * 4 + slab % 4) * 4 + z % 2 * 2 + band % 2))
    return pairs


OUTER = other_side()


def qkv_kernel(joined, meta, x0, xl, xr, xt, xb, wo, wc, wza, wzb, wca, wcb, scale_in, shift_in, qg_in, kg_in, *rest):
    if joined:
        first, q_ref, kv_ref, both_ref, wbuf, nbuf, xbuf, scale, shift, qg, kg, sems, wsems = rest
    else:
        q_ref, kv_ref, wbuf, nbuf, xbuf, scale, shift, qg, kg, sems, wsems = rest
    far = pl.ds(HALF if joined else 0, HALF)
    early = [(x0, xbuf.at[0]), (xl, xbuf.at[1]), (xr, xbuf.at[2]),
             (xt.at[far], xbuf.at[3, pl.ds(0, HALF)]), (xb.at[far], xbuf.at[3, pl.ds(HALF, HALF)]),
             (scale_in, scale), (shift_in, shift), (qg_in, qg), (kg_in, kg)]

    def krows(k):
        return pl.ds(pl.multiple_of(meta[4 + k] * FS, FS), FS)

    late = [(wo, wbuf.at[:, krows(0)]), (wc, wbuf.at[:, krows(1)]),
            (wza, wbuf.at[0:1, krows(2)]), (wzb, wbuf.at[1:3, krows(2)]),
            (wca, wbuf.at[0:1, krows(3)]), (wcb, wbuf.at[1:3, krows(3)])]
    if joined:
        late.append((first, both_ref.at[pl.ds(0, ROWS)]))
    early = [pltpu.make_async_copy(src, dst, sems.at[n]) for n, (src, dst) in enumerate(early)]
    late = [pltpu.make_async_copy(src, dst, wsems.at[n]) for n, (src, dst) in enumerate(late)]
    for copy in early + late:
        copy.start()
    for copy in early:
        copy.wait()

    step = 32

    def normalise(i, carry):
        r = pl.ds(pl.multiple_of(i * step, step), step)
        parts = [xbuf[k, r, :].astype(F32) for k in range(4)]
        total = functools.reduce(jnp.add, parts)
        center = jnp.sum(total, axis=-1, keepdims=True) * (1.0 / D)
        parts = [p - center for p in parts]
        squares = functools.reduce(jnp.add, [p * p for p in parts])
        inv = lax.rsqrt(jnp.sum(squares, axis=-1, keepdims=True) * (1.0 / D) + 1e-06)
        for k, p in enumerate(parts):
            at = meta[k]
            y = p * inv * (1.0 + scale[at]) + shift[at]
            nbuf[r, pl.ds(pl.multiple_of(at * FS, FS), FS)] = y.astype(BF16)
        return carry

    lax.fori_loop(0, ROWS // step, normalise, 0)
    for copy in late:
        copy.wait()
    for p in (1, 2, 0):
        acc = jnp.dot(nbuf[...], wbuf[p], preferred_element_type=F32)
        if p == 2:
            kv_ref[:, HF:] = acc.astype(BF16)
            continue
        gain = kg if p else qg
        for h in range(HH):
            part = acc[:, h * HD:(h + 1) * HD]
            squares = jnp.mean(part * part, axis=-1, keepdims=True)
            out = (part * lax.rsqrt(squares + 1e-06) * gain[...]).astype(BF16)
            if p:
                kv_ref[:, h * HD:(h + 1) * HD] = out
            else:
                q_ref[:, h * HD:(h + 1) * HD] = out
        if p == 0 and joined:
            both_ref[ROWS:, :] = kv_ref[...]


def qkv(meta, xs, ws, scale, shift, qg, kg, *first):
    shapes = [(ROWS, HF), (ROWS, 2 * HF)] + [(2 * ROWS, 2 * HF)] * len(first)
    return pl.pallas_call(
        functools.partial(qkv_kernel, bool(first)),
        out_shape=[jax.ShapeDtypeStruct(shape, BF16) for shape in shapes],
        in_specs=[SM] + [HBM] * (15 + len(first)),
        out_specs=[VM] * len(shapes),
        scratch_shapes=[
            pltpu.VMEM((3, D, HF), BF16),
            pltpu.VMEM((ROWS, D), BF16),
            pltpu.VMEM((4, ROWS, FS), BF16),
            pltpu.VMEM((4, 1, FS), F32),
            pltpu.VMEM((4, 1, FS), F32),
            pltpu.VMEM((1, HD), F32),
            pltpu.VMEM((1, HD), F32),
            pltpu.SemaphoreType.DMA((9,)),
            pltpu.SemaphoreType.DMA((7,)),
        ],
        compiler_params=pltpu.CompilerParams(vmem_limit_bytes=56 * 2**20),
        cost_estimate=pl.CostEstimate(flops=2 * ROWS * D * 3 * HF, bytes_accessed=10 * 2**20, transcendentals=0),
        name="qkv",
    )(meta, *xs, *ws, scale, shift, qg, kg, *first)


def attend_kernel(meta, ids, q_ref, *rest):
    pieces = rest[:10]
    o_ref, kv, sems = rest[10:]
    y = meta[11]
    jobs = []
    for cr in range(2):
        both, up, down, crossed, direct = pieces[cr * 5:cr * 5 + 5]
        at = [(t * 2 + cr) * 2 * ROWS for t in range(3)]
        jobs.append((None, both, at[1], cr * 5))
        jobs.append((y != 0, up, at[0], cr * 5 + 1))
        jobs.append((y != 3, down, at[2], cr * 5 + 2))
        for last, base in ((0, at[0]), (3, at[2])):
            jobs.append((y == last, crossed, base, cr * 5 + 3))
            jobs.append((y == last, direct, base + ROWS, cr * 5 + 4))

    def each(do):
        for condition, source, first, n in jobs:
            copy = pltpu.make_async_copy(source, kv.at[pl.ds(first, source.shape[0])], sems.at[n])
            if condition is None:
                do(copy)
            else:
                pl.when(condition)(functools.partial(do, copy))

    each(lambda copy: copy.start())
    each(lambda copy: copy.wait())
    slab, side, core = meta[8], meta[9], meta[10]

    def place(tile):
        dt = jnp.clip(tile // 12 - slab + 1, 0, 2)
        row = (tile // 3) % 4
        r = jnp.abs(row // 2 - side)
        cr = jnp.abs(row % 2 - core)
        return (((dt * 2 + cr) * 2 + r) * 3 + tile % 3) * TILE

    factor = 1.0 / HD**0.5

    def run(qt, count, slots):
        spots = [pl.multiple_of(place(ids[qt, j]), TILE) for j in range(slots)]
        rows = pl.ds(pl.multiple_of(qt * TILE, TILE), TILE)
        live = [jnp.where(j < count, 0.0, -1e30) for j in range(slots)]
        cols = [slice(h * HD, (h + 1) * HD) for h in range(HH)]
        vcols = [slice(HF + h * HD, HF + (h + 1) * HD) for h in range(HH)]
        scores = [[] for _ in range(HH)]
        for h in range(HH):
            q = q_ref[rows, cols[h]]
            for j in range(0, slots, 2):
                k = jnp.concatenate([kv[pl.ds(spots[j], TILE), cols[h]], kv[pl.ds(spots[j + 1], TILE), cols[h]]], axis=0)
                s = lax.dot_general(q, k, (((1,), (1,)), ((), ())), preferred_element_type=F32)
                for i in range(2):
                    scores[h].append(s[:, i * TILE:(i + 1) * TILE] * factor + live[j + i])
        tops = [functools.reduce(jnp.maximum, scores[h]) for h in range(HH)]
        tops = [jnp.max(t, axis=-1, keepdims=True) for t in tops]
        weights = [[jnp.exp(s - tops[h]) for s in scores[h]] for h in range(HH)]
        totals = [functools.reduce(jnp.add, weights[h]) for h in range(HH)]
        invs = [1.0 / jnp.sum(t, axis=-1, keepdims=True) for t in totals]
        outs = []
        for h in range(HH):
            acc = None
            for j in range(0, slots, 2):
                p = jnp.concatenate([(w * invs[h]).astype(BF16) for w in weights[h][j:j + 2]], axis=1)
                v = jnp.concatenate([kv[pl.ds(spots[j], TILE), vcols[h]], kv[pl.ds(spots[j + 1], TILE), vcols[h]]], axis=0)
                o = jnp.dot(p, v, preferred_element_type=F32)
                acc = o if acc is None else acc + o
            outs.append(acc.astype(BF16))
        o_ref[rows, :] = jnp.concatenate(outs, axis=1)

    def tile_loop(qt, carry):
        count = ids[qt, WIN]
        lo = 0
        for slots in (4, 8, WIN):
            @pl.when((count > lo) & (count <= slots))
            def _(slots=slots):
                run(qt, count, slots)
            lo = slots
        return carry

    lax.fori_loop(0, ROWS // TILE, tile_loop, 0)


def attend(meta, ids, q, pieces):
    return pl.pallas_call(
        attend_kernel,
        out_shape=jax.ShapeDtypeStruct((ROWS, HF), BF16),
        in_specs=[SM, SM, VM] + [ANY] * 10,
        out_specs=VM,
        scratch_shapes=[
            pltpu.VMEM((12 * ROWS, 2 * HF), BF16),
            pltpu.SemaphoreType.DMA((10,)),
        ],
        compiler_params=pltpu.CompilerParams(vmem_limit_bytes=16 * 2**20),
        cost_estimate=pl.CostEstimate(flops=4 * ROWS * WIN * TILE * HF, bytes_accessed=8 * 2**20,
                                      transcendentals=ROWS * WIN * TILE * HH),
        name="attend",
    )(meta, ids, q, *pieces)


def out_kernel(meta, home, back, w, right_ref, left_ref, keep_right, keep_left, mine_ref):
    side = meta[9]

    def product(k):
        cols = lanes(meta[k], FS)
        rows = [pl.ds(pl.multiple_of(h * HF, HF), HF) for h in (side, 1 - side)]
        return (jnp.dot(home[...], w[rows[0], cols], preferred_element_type=F32)
                + jnp.dot(back[...], w[rows[1], cols], preferred_element_type=F32))

    far = product(3)
    right_ref[:HALF, :] = far[:HALF].astype(BF16)
    left_ref[:HALF, :] = far[HALF:].astype(BF16)
    right = product(2)
    right_ref[HALF:, :] = right[HALF:].astype(BF16)
    keep_right[...] = right[:HALF]
    left = product(1)
    left_ref[HALF:, :] = left[:HALF].astype(BF16)
    keep_left[...] = left[HALF:]
    mine_ref[...] = product(0)


def out_proj(meta, home, back, w):
    return pl.pallas_call(
        out_kernel,
        out_shape=[jax.ShapeDtypeStruct((ROWS, FS), BF16)] * 2 + [jax.ShapeDtypeStruct((HALF, FS), F32)] * 2
        + [jax.ShapeDtypeStruct((ROWS, FS), F32)],
        in_specs=[SM] + [VM] * 3,
        out_specs=[VM] * 5,
        compiler_params=pltpu.CompilerParams(vmem_limit_bytes=24 * 2**20),
        cost_estimate=pl.CostEstimate(flops=2 * ROWS * D * FS, bytes_accessed=8 * 2**20, transcendentals=0),
        name="out_proj",
    )(meta, home, back, w)


def last_kernel(mine, from_left, from_right, left_sum, right_sum, gate, o_ref):
    top = mine[:HALF, :] + from_right[HALF:, :].astype(F32) + left_sum[...].astype(F32)
    o_ref[:HALF, :] = (top * gate[...]).astype(BF16)
    bottom = mine[HALF:, :] + from_left[HALF:, :].astype(F32) + right_sum[...].astype(F32)
    o_ref[HALF:, :] = (bottom * gate[...]).astype(BF16)


def last_sum(*args):
    return pl.pallas_call(
        last_kernel,
        out_shape=jax.ShapeDtypeStruct((ROWS, FS), BF16),
        in_specs=[VM] * 6,
        out_specs=VM,
        compiler_params=pltpu.CompilerParams(vmem_limit_bytes=12 * 2**20),
        name="last_sum",
    )(*args)


def lanes(k, size):
    return pl.ds(pl.multiple_of(k * size, 128), size)


def after(x, *earlier):
    return lax.optimization_barrier((x,) + earlier)[0]


UP = [(s, s + 1) for s in range(15) if s % 4 != 3]
DOWN = [(s + 1, s) for s in range(15) if s % 4 != 3]
WRAP = [(s, s + 1) for s in range(15) if s % 4 == 3] + [(s + 1, s) for s in range(15) if s % 4 == 3]
WRAP_Y = [(s, s - 3) for s in range(15) if s % 4 == 3] + [(s + 1, s + 4) for s in range(15) if s % 4 == 3]
WRAP_Z = [(s - 3, s + 1) for s in range(15) if s % 4 == 3] + [(s + 4, s) for s in range(15) if s % 4 == 3]


def shards(tokens, w_qkv, w_out, shift, scale, gate, q_gain, k_gain, tile_ids, key_counts):
    tp = lax.axis_index("tp")
    slab = lax.axis_index("slab")
    band = lax.axis_index("band")
    side, core = band // 2, band % 2
    meta = jnp.stack([
        tp, (tp + 3) % 4, (tp + 1) % 4, (tp + 2) % 4,
        band, band ^ 1, band ^ 2, band ^ 3,
        slab, side, core, slab % 4,
    ]).astype(jnp.int32)

    swap = functools.partial(lax.ppermute, axis_name="band", perm=CORE)
    pair = functools.partial(lax.ppermute, axis_name="band", perm=PAIR)

    def tp_to(x, perm):
        return lax.ppermute(x, "tp", perm)

    def slab_to(x, perm):
        return lax.ppermute(x, "slab", perm)

    partner_tokens = pair(tokens)
    xl, xr = tp_to(tokens, RIGHT), tp_to(tokens, LEFT)
    w = w_qkv.transpose(1, 0, 2)
    w_own = lax.dynamic_slice_in_dim(w, side * HF, HF, 2)
    w_away = lax.dynamic_slice_in_dim(w, (1 - side) * HF, HF, 2)
    w_zb = lax.ppermute(w_away[1:], ("slab", "band"), OUTER)
    w_za = pair(after(w_away[:1], partner_tokens))
    w_core = swap(w_own)
    passed = after(partner_tokens, xl, xr)
    pl_, pr_ = tp_to(passed, RIGHT), tp_to(passed, LEFT)
    far_top = tp_to(jnp.concatenate([xl[:HALF], pl_[:HALF]], axis=0), RIGHT)
    far_bottom = tp_to(jnp.concatenate([xr[HALF:], pr_[HALF:]], axis=0), LEFT)
    own_x = (tokens, xl, xr, far_top, far_bottom)
    partner_x = (partner_tokens, pl_, pr_, far_top, far_bottom)
    w_za, w_zb = after(w_za, pl_, pr_), after(w_zb, pl_, pr_)
    ws = [w_own, w_core, w_za, w_zb, swap(w_za), swap(w_zb)]

    scale4, shift4 = scale.reshape(4, 1, FS), shift.reshape(4, 1, FS)
    qg, kg = q_gain.reshape(1, HD), k_gain.reshape(1, HD)

    own_q, own_kv = qkv(meta, own_x, ws, scale4, shift4, qg, kg)
    crossed = slab_to(own_kv, WRAP_Y)
    partner_q, partner_kv, both = qkv(meta, partner_x, ws, scale4, shift4, qg, kg, own_kv)
    listed = jnp.concatenate([tile_ids, key_counts[:, None], key_counts[:, None]], axis=1)
    partner_listed = pair(after(listed, own_kv))
    near = [both, slab_to(both, UP), slab_to(after(both, crossed), DOWN),
            slab_to(after(crossed, partner_listed), WRAP_Z), slab_to(partner_kv, WRAP)]
    pieces = near + [swap(x) for x in near]
    away = attend(meta, partner_listed, partner_q, pieces)
    back = pair(away)
    home = attend(meta, listed, after(own_q, away), pieces)
    to_right, to_left, keep_right, keep_left, mine = out_proj(meta, home, back, w_out)
    from_left, from_right = tp_to(to_right, RIGHT), tp_to(to_left, LEFT)
    left_sum = tp_to((keep_right + from_left[:HALF].astype(F32)).astype(BF16), RIGHT)
    right_sum = tp_to((keep_left + from_right[:HALF].astype(F32)).astype(BF16), LEFT)
    return last_sum(mine, from_left, from_right, left_sum, right_sum, gate.reshape(1, FS))


def solution(mesh):
    in_specs = (
        P(("slab", "band"), "tp"),
        P("band", None, "tp"),
        P("tp", None),
        P(),
        P(),
        P("tp"),
        P(),
        P(),
        P(("slab", "band"), None),
        P(("slab", "band")),
    )
    out_specs = P(("slab", "band"), "tp")
    return jax.shard_map(shards, mesh=mesh, in_specs=in_specs, out_specs=out_specs, check_vma=False)
```

```python
import functools

import jax
import jax.numpy as jnp
from jax import lax
from jax.experimental import pallas as pl
from jax.experimental.pallas import tpu as pltpu
from jax.sharding import PartitionSpec as P

HD = 128
HH = 3
HF = HH * HD
TILE = 128
WIN = 14
ROWS = 384
HALF = ROWS // 2
FS = 768
D = 3072
F32 = jnp.float32
BF16 = jnp.bfloat16
HBM = pl.BlockSpec(memory_space=pltpu.HBM)
ANY = pl.BlockSpec(memory_space=pl.ANY)
VM = pl.BlockSpec(memory_space=pltpu.VMEM)
SM = pl.BlockSpec(memory_space=pltpu.SMEM)

RIGHT = [(i, (i + 1) % 4) for i in range(4)]
LEFT = [(i, (i + 3) % 4) for i in range(4)]
ACROSS = [(i, (i + 2) % 4) for i in range(4)]
CORE = [(b, b ^ 1) for b in range(4)]
PAIR = [(b, b ^ 2) for b in range(4)]
LATER = [(i, i + 1) for i in range(15)]
EARLIER = [(i + 1, i) for i in range(15)]


def other_side():
    pairs = []
    for slab in range(16):
        for band in range(4):
            z = (slab // 4) * 2 + band // 2
            z = (z - 1) % 8 if z % 2 == 0 else (z + 1) % 8
            pairs.append((slab * 4 + band, (z // 2 * 4 + slab % 4) * 4 + z % 2 * 2 + band % 2))
    return pairs


OUTER = other_side()


def qkv_kernel(meta, x0, xl, xr, xt, xb, wo, wc, wza, wzb, wca, wcb, scale_in, shift_in, qg_in, kg_in, *rest):
    q_ref, kv_ref, wbuf, nbuf, xbuf, scale, shift, qg, kg, sems, wsems = rest
    rows = pl.ds(0, ROWS)
    early = [(x0.at[rows], xbuf.at[0]), (xl.at[rows], xbuf.at[1]), (xr.at[rows], xbuf.at[2]),
             (xt, xbuf.at[3, pl.ds(0, HALF)]), (xb, xbuf.at[3, pl.ds(HALF, HALF)]),
             (scale_in, scale), (shift_in, shift), (qg_in, qg), (kg_in, kg)]

    def krows(k):
        return pl.ds(pl.multiple_of(meta[4 + k] * FS, FS), FS)

    late = []
    for k, parts in enumerate(((wo,), (wc,), (wza, wzb), (wca, wcb))):
        blocks = [part.at[n] for part in parts for n in range(part.shape[0])]
        late += [(block, wbuf.at[krows(k), pl.ds(p * HF, HF)]) for p, block in enumerate(blocks)]
    early = [pltpu.make_async_copy(src, dst, sems.at[n]) for n, (src, dst) in enumerate(early)]
    late = [pltpu.make_async_copy(src, dst, wsems.at[n]) for n, (src, dst) in enumerate(late)]
    for copy in early:
        copy.start()
    for copy in early:
        copy.wait()
    for copy in late:
        copy.start()

    step = 64

    def normalise(i, carry):
        r = pl.ds(pl.multiple_of(i * step, step), step)
        parts = [xbuf[k, r, :].astype(F32) for k in range(4)]
        total = functools.reduce(jnp.add, parts)
        center = jnp.sum(total, axis=-1, keepdims=True) * (1.0 / D)
        parts = [p - center for p in parts]
        squares = functools.reduce(jnp.add, [p * p for p in parts])
        inv = lax.rsqrt(jnp.sum(squares, axis=-1, keepdims=True) * (1.0 / D) + 1e-06)
        for k, p in enumerate(parts):
            at = meta[k]
            y = p * inv * (1.0 + scale[at]) + shift[at]
            nbuf[r, pl.ds(pl.multiple_of(at * FS, FS), FS)] = y.astype(BF16)
        return carry

    lax.fori_loop(0, ROWS // step, normalise, 0)
    for copy in late:
        copy.wait()
    def head_norm(part, gain):
        squares = jnp.mean(part * part, axis=-1, keepdims=True)
        return (part * lax.rsqrt(squares + 1e-06) * gain[...]).astype(BF16)

    acc = jnp.dot(nbuf[...], wbuf[...], preferred_element_type=F32)
    for h in range(HH):
        cols = slice(h * HD, (h + 1) * HD)
        q_ref[:, cols] = head_norm(acc[:, cols], qg)
        kv_ref[:, cols] = head_norm(acc[:, HF + h * HD:HF + (h + 1) * HD], kg)
    kv_ref[:, HF:] = acc[:, 2 * HF:].astype(BF16)


def join_kernel(first, second, crossed, out, sems):
    copies = [pltpu.make_async_copy(src, out.at[pl.ds(n * ROWS, ROWS)], sems.at[n]) for n, src in enumerate((first, second))]
    for copy in copies:
        copy.start()
    for copy in copies:
        copy.wait()


def join(first, second, crossed):
    return pl.pallas_call(
        join_kernel,
        out_shape=jax.ShapeDtypeStruct((2 * ROWS, 2 * HF), BF16),
        in_specs=[ANY] * 3,
        out_specs=VM,
        scratch_shapes=[pltpu.SemaphoreType.DMA((2,))],
        compiler_params=pltpu.CompilerParams(vmem_limit_bytes=4 * 2**20),
        cost_estimate=pl.CostEstimate(flops=10**11, bytes_accessed=4 * 2**20, transcendentals=0),
        name="join",
    )(first, second, crossed)


def qkv(meta, xs, ws, scale, shift, qg, kg):
    shapes = [(ROWS, HF), (ROWS, 2 * HF)]
    return pl.pallas_call(
        qkv_kernel,
        out_shape=[jax.ShapeDtypeStruct(shape, BF16) for shape in shapes],
        in_specs=[SM] + [HBM] * 15,
        out_specs=[VM] * len(shapes),
        scratch_shapes=[
            pltpu.VMEM((D, 3 * HF), BF16),
            pltpu.VMEM((ROWS, D), BF16),
            pltpu.VMEM((4, ROWS, FS), BF16),
            pltpu.VMEM((4, 1, FS), F32),
            pltpu.VMEM((4, 1, FS), F32),
            pltpu.VMEM((1, HD), F32),
            pltpu.VMEM((1, HD), F32),
            pltpu.SemaphoreType.DMA((9,)),
            pltpu.SemaphoreType.DMA((13,)),
        ],
        compiler_params=pltpu.CompilerParams(vmem_limit_bytes=56 * 2**20),
        cost_estimate=pl.CostEstimate(flops=10**11, bytes_accessed=10 * 2**20, transcendentals=0),
        name="qkv",
    )(meta, *xs, *ws, scale, shift, qg, kg)


def attend_kernel(meta, ids, q_ref, *rest):
    pieces = rest[:10]
    o_ref, kv, sems = rest[10:]
    y = meta[11]
    jobs = []
    for cr in range(2):
        both, up, down, crossed, direct = pieces[cr * 5:cr * 5 + 5]
        at = [(t * 2 + cr) * 2 * ROWS for t in range(3)]
        jobs.append((None, both, at[1], cr * 5))
        jobs.append((y != 0, up, at[0], cr * 5 + 1))
        jobs.append((y != 3, down, at[2], cr * 5 + 2))
        for last, base in ((0, at[0]), (3, at[2])):
            jobs.append((y == last, crossed, base, cr * 5 + 3))
            jobs.append((y == last, direct, base + ROWS, cr * 5 + 4))

    def each(do):
        for condition, source, first, n in jobs:
            copy = pltpu.make_async_copy(source, kv.at[pl.ds(first, source.shape[0])], sems.at[n])
            if condition is None:
                do(copy)
            else:
                pl.when(condition)(functools.partial(do, copy))

    each(lambda copy: copy.start())
    each(lambda copy: copy.wait())
    slab, side, core = meta[8], meta[9], meta[10]

    def place(tile):
        dt = jnp.clip(tile // 12 - slab + 1, 0, 2)
        row = (tile // 3) % 4
        r = jnp.abs(row // 2 - side)
        cr = jnp.abs(row % 2 - core)
        return (((dt * 2 + cr) * 2 + r) * 3 + tile % 3) * TILE

    factor = 1.0 / HD**0.5

    def run(qt, count, slots):
        spots = [pl.multiple_of(place(ids[qt, j]), TILE) for j in range(slots)]
        rows = pl.ds(pl.multiple_of(qt * TILE, TILE), TILE)
        live = [jnp.where(j < count, 0.0, -1e30) for j in range(slots)]
        cols = [slice(h * HD, (h + 1) * HD) for h in range(HH)]
        vcols = [slice(HF + h * HD, HF + (h + 1) * HD) for h in range(HH)]
        scores = [[] for _ in range(HH)]
        for h in range(HH):
            q = q_ref[rows, cols[h]]
            for j in range(0, slots, 2):
                k = jnp.concatenate([kv[pl.ds(spots[j], TILE), cols[h]], kv[pl.ds(spots[j + 1], TILE), cols[h]]], axis=0)
                s = lax.dot_general(q, k, (((1,), (1,)), ((), ())), preferred_element_type=F32)
                for i in range(2):
                    scores[h].append(s[:, i * TILE:(i + 1) * TILE] * factor + live[j + i])
        tops = [functools.reduce(jnp.maximum, scores[h]) for h in range(HH)]
        tops = [jnp.max(t, axis=-1, keepdims=True) for t in tops]
        weights = [[jnp.exp(s - tops[h]) for s in scores[h]] for h in range(HH)]
        totals = [functools.reduce(jnp.add, weights[h]) for h in range(HH)]
        invs = [1.0 / jnp.sum(t, axis=-1, keepdims=True) for t in totals]
        outs = []
        for h in range(HH):
            acc = None
            for j in range(0, slots, 2):
                p = jnp.concatenate([(w * invs[h]).astype(BF16) for w in weights[h][j:j + 2]], axis=1)
                v = jnp.concatenate([kv[pl.ds(spots[j], TILE), vcols[h]], kv[pl.ds(spots[j + 1], TILE), vcols[h]]], axis=0)
                o = jnp.dot(p, v, preferred_element_type=F32)
                acc = o if acc is None else acc + o
            outs.append(acc.astype(BF16))
        o_ref[rows, :] = jnp.concatenate(outs, axis=1)

    def tile_loop(qt, carry):
        count = ids[qt, WIN]
        lo = 0
        for slots in (4, 8, WIN):
            @pl.when((count > lo) & (count <= slots))
            def _(slots=slots):
                run(qt, count, slots)
            lo = slots
        return carry

    lax.fori_loop(0, ROWS // TILE, tile_loop, 0)


def attend(meta, ids, q, pieces):
    return pl.pallas_call(
        attend_kernel,
        out_shape=jax.ShapeDtypeStruct((ROWS, HF), BF16),
        in_specs=[SM, SM, VM] + [ANY] * 10,
        out_specs=VM,
        scratch_shapes=[
            pltpu.VMEM((12 * ROWS, 2 * HF), BF16),
            pltpu.SemaphoreType.DMA((10,)),
        ],
        compiler_params=pltpu.CompilerParams(vmem_limit_bytes=16 * 2**20),
        cost_estimate=pl.CostEstimate(flops=4 * ROWS * WIN * TILE * HF, bytes_accessed=8 * 2**20,
                                      transcendentals=ROWS * WIN * TILE * HH),
        name="attend",
    )(meta, ids, q, *pieces)


def out_kernel(meta, home, back, w, right_ref, left_ref, keep_right, keep_left, mine_ref):
    side = meta[9]

    def product(k):
        cols = lanes(meta[k], FS)
        rows = [pl.ds(pl.multiple_of(h * HF, HF), HF) for h in (side, 1 - side)]
        return (jnp.dot(home[...], w[rows[0], cols], preferred_element_type=F32)
                + jnp.dot(back[...], w[rows[1], cols], preferred_element_type=F32))

    far = product(3)
    right_ref[:HALF, :] = far[:HALF].astype(BF16)
    left_ref[:HALF, :] = far[HALF:].astype(BF16)
    right = product(2)
    right_ref[HALF:, :] = right[HALF:].astype(BF16)
    keep_right[...] = right[:HALF]
    left = product(1)
    left_ref[HALF:, :] = left[:HALF].astype(BF16)
    keep_left[...] = left[HALF:]
    mine_ref[...] = product(0)


def out_proj(meta, home, back, w):
    return pl.pallas_call(
        out_kernel,
        out_shape=[jax.ShapeDtypeStruct((ROWS, FS), BF16)] * 2 + [jax.ShapeDtypeStruct((HALF, FS), F32)] * 2
        + [jax.ShapeDtypeStruct((ROWS, FS), F32)],
        in_specs=[SM] + [VM] * 3,
        out_specs=[VM] * 5,
        compiler_params=pltpu.CompilerParams(vmem_limit_bytes=24 * 2**20),
        cost_estimate=pl.CostEstimate(flops=2 * ROWS * D * FS, bytes_accessed=8 * 2**20, transcendentals=0),
        name="out_proj",
    )(meta, home, back, w)


def last_kernel(mine, from_left, from_right, left_sum, right_sum, gate, o_ref):
    top = mine[:HALF, :] + from_right[HALF:, :].astype(F32) + left_sum[...].astype(F32)
    o_ref[:HALF, :] = (top * gate[...]).astype(BF16)
    bottom = mine[HALF:, :] + from_left[HALF:, :].astype(F32) + right_sum[...].astype(F32)
    o_ref[HALF:, :] = (bottom * gate[...]).astype(BF16)


def last_sum(*args):
    return pl.pallas_call(
        last_kernel,
        out_shape=jax.ShapeDtypeStruct((ROWS, FS), BF16),
        in_specs=[VM] * 6,
        out_specs=VM,
        compiler_params=pltpu.CompilerParams(vmem_limit_bytes=12 * 2**20),
        name="last_sum",
    )(*args)


def lanes(k, size):
    return pl.ds(pl.multiple_of(k * size, 128), size)


def after(x, *earlier):
    return lax.optimization_barrier((x,) + earlier)[0]


UP = [(s, s + 1) for s in range(15) if s % 4 != 3]
DOWN = [(s + 1, s) for s in range(15) if s % 4 != 3]
WRAP = [(s, s + 1) for s in range(15) if s % 4 == 3] + [(s + 1, s) for s in range(15) if s % 4 == 3]
WRAP_Y = [(s, s - 3) for s in range(15) if s % 4 == 3] + [(s + 1, s + 4) for s in range(15) if s % 4 == 3]
WRAP_Z = [(s - 3, s + 1) for s in range(15) if s % 4 == 3] + [(s + 4, s) for s in range(15) if s % 4 == 3]


def shards(tokens, w_qkv, w_out, shift, scale, gate, q_gain, k_gain, tile_ids, key_counts):
    tp = lax.axis_index("tp")
    slab = lax.axis_index("slab")
    band = lax.axis_index("band")
    side, core = band // 2, band % 2
    meta = jnp.stack([
        tp, (tp + 3) % 4, (tp + 1) % 4, (tp + 2) % 4,
        band, band ^ 1, band ^ 2, band ^ 3,
        slab, side, core, slab % 4,
    ]).astype(jnp.int32)

    swap = functools.partial(lax.ppermute, axis_name="band", perm=CORE)
    pair = functools.partial(lax.ppermute, axis_name="band", perm=PAIR)

    def tp_to(x, perm):
        return lax.ppermute(x, "tp", perm)

    def slab_to(x, perm):
        return lax.ppermute(x, "slab", perm)

    xl, xr = tp_to(tokens, RIGHT), tp_to(tokens, LEFT)
    listed = jnp.concatenate([tile_ids, key_counts[:, None], key_counts[:, None]], axis=1)
    below = jnp.pad(listed.astype(BF16), ((0, 13), (0, FS - WIN - 2)))
    partner_all = pair(jnp.concatenate([tokens, below], axis=0))
    partner_listed = partner_all[ROWS:ROWS + 3, :WIN + 2].astype(jnp.int32)
    w = w_qkv.transpose(1, 0, 2)
    w_own = lax.dynamic_slice_in_dim(w, side * HF, HF, 2)
    w_away = lax.dynamic_slice_in_dim(w, (1 - side) * HF, HF, 2)
    w_zb = lax.ppermute(w_away[1:], ("slab", "band"), OUTER)
    w_za = pair(after(w_away[:1], partner_all))
    w_core = swap(w_own)
    xt, xb = tp_to(xl[:HALF], RIGHT), tp_to(xr[HALF:], LEFT)
    passed = after(partner_all, xt, xb)
    pl_, pr_ = tp_to(passed, RIGHT), tp_to(passed, LEFT)
    w_za, w_zb = after(w_za, xt, xb), after(w_zb, xt, xb)
    ws = [after(w_own, pl_, pr_), w_core, w_za, w_zb, swap(w_za), swap(w_zb)]

    scale4, shift4 = scale.reshape(4, 1, FS), shift.reshape(4, 1, FS)
    qg, kg = q_gain.reshape(1, HD), k_gain.reshape(1, HD)

    own_q, own_kv = qkv(meta, (tokens, xl, xr, xt, xb), ws, scale4, shift4, qg, kg)
    crossed = slab_to(own_kv, WRAP_Y)
    pt, pb = tp_to(pl_[:HALF], RIGHT), tp_to(pr_[HALF:ROWS], LEFT)
    partner_q, partner_kv = qkv(meta, (partner_all, pl_, pr_, pt, pb), ws, scale4, shift4, qg, kg)
    second, direct = slab_to(crossed, WRAP_Z), slab_to(partner_kv, WRAP)
    both = join(own_kv, partner_kv, crossed)
    wrapped = [second, direct, swap(second), swap(direct)]
    up, down = after(slab_to(both, UP), *wrapped), after(slab_to(both, DOWN), *wrapped)
    pieces = [both, up, down, second, direct, swap(both), swap(up), swap(down)] + wrapped[2:]
    away = attend(meta, partner_listed, partner_q, pieces)
    back = pair(away)
    home = attend(meta, listed, after(own_q, away), pieces)
    to_right, to_left, keep_right, keep_left, mine = out_proj(meta, home, back, w_out)
    from_left, from_right = tp_to(to_right, RIGHT), tp_to(to_left, LEFT)
    left_sum = tp_to((keep_right + from_left[:HALF].astype(F32)).astype(BF16), RIGHT)
    right_sum = tp_to((keep_left + from_right[:HALF].astype(F32)).astype(BF16), LEFT)
    return last_sum(mine, from_left, from_right, left_sum, right_sum, gate.reshape(1, FS))


def solution(mesh):
    in_specs = (
        P(("slab", "band"), "tp"),
        P("band", None, "tp"),
        P("tp", None),
        P(),
        P(),
        P("tp"),
        P(),
        P(),
        P(("slab", "band"), None),
        P(("slab", "band")),
    )
    out_specs = P(("slab", "band"), "tp")
    return jax.shard_map(shards, mesh=mesh, in_specs=in_specs, out_specs=out_specs, check_vma=False)
```

```python
import functools

import jax
import jax.numpy as jnp
from jax import lax
from jax.experimental import pallas as pl
from jax.experimental.pallas import tpu as pltpu
from jax.sharding import PartitionSpec as P

HD = 128
HH = 3
HF = HH * HD
TILE = 128
WIN = 14
ROWS = 384
HALF = ROWS // 2
FS = 768
D = 3072
F32 = jnp.float32
BF16 = jnp.bfloat16
HBM = pl.BlockSpec(memory_space=pltpu.HBM)
ANY = pl.BlockSpec(memory_space=pl.ANY)
VM = pl.BlockSpec(memory_space=pltpu.VMEM)
SM = pl.BlockSpec(memory_space=pltpu.SMEM)

RIGHT = [(i, (i + 1) % 4) for i in range(4)]
LEFT = [(i, (i + 3) % 4) for i in range(4)]
ACROSS = [(i, (i + 2) % 4) for i in range(4)]
CORE = [(b, b ^ 1) for b in range(4)]
PAIR = [(b, b ^ 2) for b in range(4)]
LATER = [(i, i + 1) for i in range(15)]
EARLIER = [(i + 1, i) for i in range(15)]


def other_side():
    pairs = []
    for slab in range(16):
        for band in range(4):
            z = (slab // 4) * 2 + band // 2
            z = (z - 1) % 8 if z % 2 == 0 else (z + 1) % 8
            pairs.append((slab * 4 + band, (z // 2 * 4 + slab % 4) * 4 + z % 2 * 2 + band % 2))
    return pairs


OUTER = other_side()


def qkv_kernel(meta, x0, xl, xr, xt, xb, wo, wc, wza, wzb, wca, wcb, scale_in, shift_in, qg_in, kg_in, *rest):
    q_ref, kv_ref, wbuf, nbuf, xbuf, scale, shift, qg, kg, sems, wsems = rest
    rows = pl.ds(0, ROWS)
    early = [(x0.at[rows], xbuf.at[0]), (xl.at[rows], xbuf.at[1]), (xr.at[rows], xbuf.at[2]),
             (xt, xbuf.at[3, pl.ds(0, HALF)]), (xb, xbuf.at[3, pl.ds(HALF, HALF)]),
             (scale_in, scale), (shift_in, shift), (qg_in, qg), (kg_in, kg)]

    def krows(k):
        return pl.ds(pl.multiple_of(meta[4 + k] * FS, FS), FS)

    late = []
    for k, parts in enumerate(((wo,), (wc,), (wza, wzb), (wca, wcb))):
        blocks = [part.at[n] for part in parts for n in range(part.shape[0])]
        late += [(block, wbuf.at[krows(k), pl.ds(p * HF, HF)]) for p, block in enumerate(blocks)]
    early = [pltpu.make_async_copy(src, dst, sems.at[n]) for n, (src, dst) in enumerate(early)]
    late = [pltpu.make_async_copy(src, dst, wsems.at[n]) for n, (src, dst) in enumerate(late)]
    for copy in early:
        copy.start()
    for copy in early:
        copy.wait()
    for copy in late:
        copy.start()

    step = 64

    def normalise(i, carry):
        r = pl.ds(pl.multiple_of(i * step, step), step)
        parts = [xbuf[k, r, :].astype(F32) for k in range(4)]
        total = functools.reduce(jnp.add, parts)
        center = jnp.sum(total, axis=-1, keepdims=True) * (1.0 / D)
        parts = [p - center for p in parts]
        squares = functools.reduce(jnp.add, [p * p for p in parts])
        inv = lax.rsqrt(jnp.sum(squares, axis=-1, keepdims=True) * (1.0 / D) + 1e-06)
        for k, p in enumerate(parts):
            at = meta[k]
            y = p * inv * (1.0 + scale[at]) + shift[at]
            nbuf[r, pl.ds(pl.multiple_of(at * FS, FS), FS)] = y.astype(BF16)
        return carry

    lax.fori_loop(0, ROWS // step, normalise, 0)
    for copy in late:
        copy.wait()
    def head_norm(part, gain):
        squares = jnp.mean(part * part, axis=-1, keepdims=True)
        return (part * lax.rsqrt(squares + 1e-06) * gain[...]).astype(BF16)

    acc = jnp.dot(nbuf[...], wbuf[...], preferred_element_type=F32)
    for h in range(HH):
        cols = slice(h * HD, (h + 1) * HD)
        q_ref[:, cols] = head_norm(acc[:, cols], qg)
        kv_ref[:, cols] = head_norm(acc[:, HF + h * HD:HF + (h + 1) * HD], kg)
    kv_ref[:, HF:] = acc[:, 2 * HF:].astype(BF16)


def join_kernel(first, second, crossed, out, sems):
    copies = [pltpu.make_async_copy(src, out.at[pl.ds(n * ROWS, ROWS)], sems.at[n]) for n, src in enumerate((first, second))]
    for copy in copies:
        copy.start()
    for copy in copies:
        copy.wait()


def join(first, second, crossed):
    return pl.pallas_call(
        join_kernel,
        out_shape=jax.ShapeDtypeStruct((2 * ROWS, 2 * HF), BF16),
        in_specs=[ANY] * 3,
        out_specs=VM,
        scratch_shapes=[pltpu.SemaphoreType.DMA((2,))],
        compiler_params=pltpu.CompilerParams(vmem_limit_bytes=4 * 2**20),
        cost_estimate=pl.CostEstimate(flops=10**11, bytes_accessed=4 * 2**20, transcendentals=0),
        name="join",
    )(first, second, crossed)


def qkv(meta, xs, ws, scale, shift, qg, kg):
    shapes = [(ROWS, HF), (ROWS, 2 * HF)]
    return pl.pallas_call(
        qkv_kernel,
        out_shape=[jax.ShapeDtypeStruct(shape, BF16) for shape in shapes],
        in_specs=[SM] + [HBM] * 15,
        out_specs=[VM] * len(shapes),
        scratch_shapes=[
            pltpu.VMEM((D, 3 * HF), BF16),
            pltpu.VMEM((ROWS, D), BF16),
            pltpu.VMEM((4, ROWS, FS), BF16),
            pltpu.VMEM((4, 1, FS), F32),
            pltpu.VMEM((4, 1, FS), F32),
            pltpu.VMEM((1, HD), F32),
            pltpu.VMEM((1, HD), F32),
            pltpu.SemaphoreType.DMA((9,)),
            pltpu.SemaphoreType.DMA((13,)),
        ],
        compiler_params=pltpu.CompilerParams(vmem_limit_bytes=56 * 2**20),
        cost_estimate=pl.CostEstimate(flops=10**11, bytes_accessed=10 * 2**20, transcendentals=0),
        name="qkv",
    )(meta, *xs, *ws, scale, shift, qg, kg)


def attend_kernel(meta, ids, q_ref, *rest):
    pieces = rest[:10]
    o_ref, kv, sems = rest[10:]
    y = meta[11]
    jobs = []
    for cr in range(2):
        both, up, down, crossed, direct = pieces[cr * 5:cr * 5 + 5]
        at = [(t * 2 + cr) * 2 * ROWS for t in range(3)]
        jobs.append((None, both, at[1], cr * 5))
        jobs.append((y != 0, up, at[0], cr * 5 + 1))
        jobs.append((y != 3, down, at[2], cr * 5 + 2))
        for last, base in ((0, at[0]), (3, at[2])):
            jobs.append((y == last, crossed, base, cr * 5 + 3))
            jobs.append((y == last, direct, base + ROWS, cr * 5 + 4))

    def each(do):
        for condition, source, first, n in jobs:
            copy = pltpu.make_async_copy(source, kv.at[pl.ds(first, source.shape[0])], sems.at[n])
            if condition is None:
                do(copy)
            else:
                pl.when(condition)(functools.partial(do, copy))

    each(lambda copy: copy.start())
    each(lambda copy: copy.wait())
    slab, side, core = meta[8], meta[9], meta[10]

    def place(tile):
        dt = jnp.clip(tile // 12 - slab + 1, 0, 2)
        row = (tile // 3) % 4
        r = jnp.abs(row // 2 - side)
        cr = jnp.abs(row % 2 - core)
        return (((dt * 2 + cr) * 2 + r) * 3 + tile % 3) * TILE

    factor = 1.0 / HD**0.5

    def run(qt, count, slots):
        spots = [pl.multiple_of(place(ids[qt, j]), TILE) for j in range(slots)]
        rows = pl.ds(pl.multiple_of(qt * TILE, TILE), TILE)
        live = [jnp.where(j < count, 0.0, -1e30) for j in range(slots)]
        cols = [slice(h * HD, (h + 1) * HD) for h in range(HH)]
        vcols = [slice(HF + h * HD, HF + (h + 1) * HD) for h in range(HH)]
        scores = [[] for _ in range(HH)]
        for h in range(HH):
            q = q_ref[rows, cols[h]]
            for j in range(0, slots, 2):
                k = jnp.concatenate([kv[pl.ds(spots[j], TILE), cols[h]], kv[pl.ds(spots[j + 1], TILE), cols[h]]], axis=0)
                s = lax.dot_general(q, k, (((1,), (1,)), ((), ())), preferred_element_type=F32)
                for i in range(2):
                    scores[h].append(s[:, i * TILE:(i + 1) * TILE] * factor + live[j + i])
        tops = [functools.reduce(jnp.maximum, scores[h]) for h in range(HH)]
        tops = [jnp.max(t, axis=-1, keepdims=True) for t in tops]
        weights = [[jnp.exp(s - tops[h]) for s in scores[h]] for h in range(HH)]
        totals = [functools.reduce(jnp.add, weights[h]) for h in range(HH)]
        invs = [1.0 / jnp.sum(t, axis=-1, keepdims=True) for t in totals]
        outs = []
        for h in range(HH):
            acc = None
            for j in range(0, slots, 2):
                p = jnp.concatenate([(w * invs[h]).astype(BF16) for w in weights[h][j:j + 2]], axis=1)
                v = jnp.concatenate([kv[pl.ds(spots[j], TILE), vcols[h]], kv[pl.ds(spots[j + 1], TILE), vcols[h]]], axis=0)
                o = jnp.dot(p, v, preferred_element_type=F32)
                acc = o if acc is None else acc + o
            outs.append(acc.astype(BF16))
        o_ref[rows, :] = jnp.concatenate(outs, axis=1)

    def tile_loop(qt, carry):
        count = ids[qt, WIN]
        lo = 0
        for slots in (4, 8, WIN):
            @pl.when((count > lo) & (count <= slots))
            def _(slots=slots):
                run(qt, count, slots)
            lo = slots
        return carry

    lax.fori_loop(0, ROWS // TILE, tile_loop, 0)


def attend(meta, ids, q, pieces):
    return pl.pallas_call(
        attend_kernel,
        out_shape=jax.ShapeDtypeStruct((ROWS, HF), BF16),
        in_specs=[SM, SM, VM] + [ANY] * 10,
        out_specs=VM,
        scratch_shapes=[
            pltpu.VMEM((12 * ROWS, 2 * HF), BF16),
            pltpu.SemaphoreType.DMA((10,)),
        ],
        compiler_params=pltpu.CompilerParams(vmem_limit_bytes=16 * 2**20),
        cost_estimate=pl.CostEstimate(flops=4 * ROWS * WIN * TILE * HF, bytes_accessed=8 * 2**20,
                                      transcendentals=ROWS * WIN * TILE * HH),
        name="attend",
    )(meta, ids, q, *pieces)


def out_kernel(meta, home, back, w, right_ref, left_ref, keep_right, keep_left, mine_ref):
    side = meta[9]

    def product(k):
        cols = lanes(meta[k], FS)
        rows = [pl.ds(pl.multiple_of(h * HF, HF), HF) for h in (side, 1 - side)]
        return (jnp.dot(home[...], w[rows[0], cols], preferred_element_type=F32)
                + jnp.dot(back[...], w[rows[1], cols], preferred_element_type=F32))

    far = product(3)
    right_ref[:HALF, :] = far[:HALF].astype(BF16)
    left_ref[:HALF, :] = far[HALF:].astype(BF16)
    right = product(2)
    right_ref[HALF:, :] = right[HALF:].astype(BF16)
    keep_right[...] = right[:HALF]
    left = product(1)
    left_ref[HALF:, :] = left[:HALF].astype(BF16)
    keep_left[...] = left[HALF:]
    mine_ref[...] = product(0)


def out_proj(meta, home, back, w):
    return pl.pallas_call(
        out_kernel,
        out_shape=[jax.ShapeDtypeStruct((ROWS, FS), BF16)] * 2 + [jax.ShapeDtypeStruct((HALF, FS), F32)] * 2
        + [jax.ShapeDtypeStruct((ROWS, FS), F32)],
        in_specs=[SM] + [VM] * 3,
        out_specs=[VM] * 5,
        compiler_params=pltpu.CompilerParams(vmem_limit_bytes=24 * 2**20),
        cost_estimate=pl.CostEstimate(flops=2 * ROWS * D * FS, bytes_accessed=8 * 2**20, transcendentals=0),
        name="out_proj",
    )(meta, home, back, w)


def last_kernel(mine, from_left, from_right, left_sum, right_sum, gate, o_ref):
    top = mine[:HALF, :] + from_right[HALF:, :].astype(F32) + left_sum[...].astype(F32)
    o_ref[:HALF, :] = (top * gate[...]).astype(BF16)
    bottom = mine[HALF:, :] + from_left[HALF:, :].astype(F32) + right_sum[...].astype(F32)
    o_ref[HALF:, :] = (bottom * gate[...]).astype(BF16)


def last_sum(*args):
    return pl.pallas_call(
        last_kernel,
        out_shape=jax.ShapeDtypeStruct((ROWS, FS), BF16),
        in_specs=[VM] * 6,
        out_specs=VM,
        compiler_params=pltpu.CompilerParams(vmem_limit_bytes=12 * 2**20),
        name="last_sum",
    )(*args)


def lanes(k, size):
    return pl.ds(pl.multiple_of(k * size, 128), size)


def after(x, *earlier):
    return lax.optimization_barrier((x,) + earlier)[0]


UP = [(s, s + 1) for s in range(15) if s % 4 != 3]
DOWN = [(s + 1, s) for s in range(15) if s % 4 != 3]
WRAP = [(s, s + 1) for s in range(15) if s % 4 == 3] + [(s + 1, s) for s in range(15) if s % 4 == 3]
WRAP_Y = [(s, s - 3) for s in range(15) if s % 4 == 3] + [(s + 1, s + 4) for s in range(15) if s % 4 == 3]
WRAP_Z = [(s - 3, s + 1) for s in range(15) if s % 4 == 3] + [(s + 4, s) for s in range(15) if s % 4 == 3]


def shards(tokens, w_qkv, w_out, shift, scale, gate, q_gain, k_gain, tile_ids, key_counts):
    tp = lax.axis_index("tp")
    slab = lax.axis_index("slab")
    band = lax.axis_index("band")
    side, core = band // 2, band % 2
    meta = jnp.stack([
        tp, (tp + 3) % 4, (tp + 1) % 4, (tp + 2) % 4,
        band, band ^ 1, band ^ 2, band ^ 3,
        slab, side, core, slab % 4,
    ]).astype(jnp.int32)

    swap = functools.partial(lax.ppermute, axis_name="band", perm=CORE)
    pair = functools.partial(lax.ppermute, axis_name="band", perm=PAIR)

    def tp_to(x, perm):
        return lax.ppermute(x, "tp", perm)

    def slab_to(x, perm):
        return lax.ppermute(x, "slab", perm)

    xl, xr = tp_to(tokens, RIGHT), tp_to(tokens, LEFT)
    listed = jnp.concatenate([tile_ids, key_counts[:, None], key_counts[:, None]], axis=1)
    below = jnp.pad(listed.astype(BF16), ((0, 13), (0, FS - WIN - 2)))
    partner_all = pair(jnp.concatenate([tokens, below], axis=0))
    partner_listed = partner_all[ROWS:ROWS + 3, :WIN + 2].astype(jnp.int32)
    w = w_qkv.transpose(1, 0, 2)
    w_own = lax.dynamic_slice_in_dim(w, side * HF, HF, 2)
    away = (1 - side) * HF
    w_zb = lax.ppermute(lax.dynamic_slice(w, (1, 0, away), (2, FS, HF)), ("slab", "band"), OUTER)
    w_za = pair(after(lax.dynamic_slice(w, (0, 0, away), (1, FS, HF)), partner_all, partner_listed))
    w_core = swap(w_own)
    xt, xb = tp_to(xl[:HALF], RIGHT), tp_to(xr[HALF:], LEFT)
    passed = after(partner_all, xt, xb)
    pl_, pr_ = tp_to(passed, RIGHT), tp_to(passed, LEFT)
    w_za, w_zb = after(w_za, xt, xb), after(w_zb, xt, xb)
    ws = [after(w_own, pl_, pr_), w_core, w_za, w_zb, swap(w_za), swap(w_zb)]

    scale4, shift4 = scale.reshape(4, 1, FS), shift.reshape(4, 1, FS)
    qg, kg = q_gain.reshape(1, HD), k_gain.reshape(1, HD)

    own_q, own_kv = qkv(meta, (tokens, xl, xr, xt, xb), ws, scale4, shift4, qg, kg)
    crossed = slab_to(own_kv, WRAP_Y)
    pt, pb = tp_to(pl_[:HALF], RIGHT), tp_to(pr_[HALF:ROWS], LEFT)
    partner_q, partner_kv = qkv(meta, (partner_all, pl_, pr_, pt, pb), ws, scale4, shift4, qg, kg)
    second, direct = slab_to(crossed, WRAP_Z), slab_to(partner_kv, WRAP)
    both = join(own_kv, partner_kv, crossed)
    wrapped = [second, direct, swap(second), swap(direct)]
    up, down = after(slab_to(both, UP), *wrapped), after(slab_to(both, DOWN), *wrapped)
    pieces = [both, up, down, second, direct, swap(both), swap(up), swap(down)] + wrapped[2:]
    away = attend(meta, partner_listed, partner_q, pieces)
    back = pair(away)
    home = attend(meta, listed, after(own_q, away), pieces)
    to_right, to_left, keep_right, keep_left, mine = out_proj(meta, home, back, w_out)
    from_left, from_right = tp_to(to_right, RIGHT), tp_to(to_left, LEFT)
    left_sum = tp_to((keep_right + from_left[:HALF].astype(F32)).astype(BF16), RIGHT)
    right_sum = tp_to((keep_left + from_right[:HALF].astype(F32)).astype(BF16), LEFT)
    return last_sum(mine, from_left, from_right, left_sum, right_sum, gate.reshape(1, FS))


def solution(mesh):
    in_specs = (
        P(("slab", "band"), "tp"),
        P("band", None, "tp"),
        P("tp", None),
        P(),
        P(),
        P("tp"),
        P(),
        P(),
        P(("slab", "band"), None),
        P(("slab", "band")),
    )
    out_specs = P(("slab", "band"), "tp")
    return jax.shard_map(shards, mesh=mesh, in_specs=in_specs, out_specs=out_specs, check_vma=False)
```
